32 devices in a mesh: clips: 2 (over x), patch: 16 (over z, y, core).
Axes of the slice: x: 2, y: 2, z: 4, core: 2. Of those that a mesh axis runs over, the one named last changes fastest.
Arguments:
- q_video: bfloat16 [2304, 1536], P(('clips', 'patch')), parts along dimension 0, may hold values from -6 to 6
- k_video: bfloat16 [2304, 1536], P(('clips', 'patch')), parts along dimension 0, may hold values from -6 to 6
- v_video: bfloat16 [2304, 1536], P(('clips', 'patch')), parts along dimension 0, may hold values from -6 to 6
- k_stale: bfloat16 [2304, 1536], P(('clips', 'patch')), parts along dimension 0, may hold values from -6 to 6
- v_stale: bfloat16 [2304, 1536], P(('clips', 'patch')), parts along dimension 0, may hold values from -6 to 6
- q_text: bfloat16 [128, 1536], P(('clips', 'patch')), parts along dimension 0, may hold values from -6 to 6
- k_text: bfloat16 [128, 1536], P(('clips', 'patch')), parts along dimension 0, may hold values from -6 to 6
- v_text: bfloat16 [128, 1536], P(('clips', 'patch')), parts along dimension 0, may hold values from -6 to 6
- q_gain: float32 [128], replicated, may hold values from 0.6 to 4
- k_gain: float32 [128], replicated, may hold values from 0.6 to 4
- out_weight: bfloat16 [1536, 3072], replicated, may hold values from -0.15625 to 0.15625
Outputs:
- video_out: bfloat16 [2304, 3072], P(('clips', 'patch')), parts along dimension 0
- text_out: bfloat16 [128, 3072], P(('clips', 'patch')), parts along dimension 0
The draws below stay inside these ranges and needn't reach their ends.
There are 2 independent parts, one for each index of `clips`. The reference program is written for one: setup_inputs(seed, part) draws one part's arguments, and reference() takes and returns one part's arrays. A program takes and returns all parts, laid end to end along the dimension named above; an argument that names none is the same for every part. Nothing has to cross between parts.
All inputs are finite; a program needn't handle non-finite values.
Results may differ from the reference program's by a relative error of at most 0.012.
The reference program's roundings to bfloat16 on the way count: a program that leaves them out, or rounds other values in their place, can miss the bound.
Values may be sent and summed in bfloat16 or wider, within the bound.
A program may use at most 128 MiB of HBM per device.

```python
import jax
import jax.numpy as jnp
from jax import lax

D = 3072
HEADS = 12
HD = 128
TOK_DEV = 72
TXT_DEV = 4
HK = 1536
TOKENS = 1152
TEXT = 64
N_PATCH = 16


def shared_keys(key):
    return jax.random.normal(key, (TOKENS, HEADS * HD), jnp.float32)


def draw_k_stale(key, part):
    base = shared_keys(key)
    return jnp.clip(base, -6.0, 6.0).astype(jnp.bfloat16)


def draw_q_video(key, part):
    key = jax.random.fold_in(key, 5)
    own = jax.random.normal(key, (TOKENS, HEADS * HD), jnp.float32)
    return jnp.clip(own, -6.0, 6.0).astype(jnp.float32).astype(jnp.bfloat16)


def gains(key):
    low = jnp.log(jnp.float32(0.6))
    high = jnp.log(jnp.float32(1.8))
    return jnp.exp(jax.random.uniform(key, (HD,), jnp.float32, low, high))


def draw_q_gain(key, part):
    key = jax.random.fold_in(key, 7)
    return gains(key)


def draw_k_gain(key, part):
    key = jax.random.fold_in(key, 9)
    return gains(key)


def level_of(key, extent, split, low, high):
    factor_of, own = 1.0, jax.random.fold_in(key, 6)
    for dim, blocks in split:
        draws = jnp.exp(jax.random.uniform(jax.random.fold_in(own, dim), (blocks,), jnp.float32, low / len(split), high / len(split)))
        factor_of = factor_of * jnp.repeat(draws, extent[dim] // blocks).reshape([-1 if axis == dim else 1 for axis in range(len(extent))])
    return factor_of


def centred(key, dims, deviation, reach, cuts=(), kind=jnp.bfloat16):
    level = level_of(key, dims, cuts, -0.22, 0.18) if cuts else 1.0
    result = jax.random.normal(key, dims, jnp.float32) * deviation * level
    return jnp.minimum(jnp.maximum(result, -reach), reach).astype(kind)


def setup_inputs(seed: int = 0, part: int = 0) -> dict:
    key_of = jax.random.split(jax.random.key(seed), 12)
    own_keys = jax.random.split(jax.random.fold_in(key_of[11], part), 12)
    return {
        "q_video": draw_q_video(jax.random.fold_in(jax.random.fold_in(key_of[11], part), 71), part),
        "k_video": centred(own_keys[1], (TOKENS, HK), 1.0, 6.0, ((0, 16),)),
        "v_video": centred(own_keys[2], (TOKENS, HK), 1.0, 6.0, ((0, 16),)),
        "k_stale": draw_k_stale(jax.random.fold_in(jax.random.fold_in(key_of[11], part), 71), part),
        "v_stale": centred(own_keys[4], (TOKENS, HK), 1.0, 6.0, ((0, 16),)),
        "q_text": centred(own_keys[5], (TEXT, HK), 1.0, 6.0, ((0, 16),)),
        "k_text": centred(own_keys[6], (TEXT, HK), 1.0, 6.0, ((0, 16),)),
        "v_text": centred(own_keys[7], (TEXT, HK), 1.0, 6.0, ((0, 16),)),
        "q_gain": draw_q_gain(jax.random.fold_in(key_of[11], 71), part),
        "k_gain": draw_k_gain(jax.random.fold_in(key_of[11], 71), part),
        "out_weight": centred(key_of[10], (HK, D), HK ** -0.5, 0.15625),
    }


def normed(rows, gain):
    heads = rows.astype(jnp.float32).reshape(rows.shape[0], -1, gain.shape[0])
    scaled = heads * lax.rsqrt(lax.optimization_barrier(jnp.mean(heads * heads, axis=-1, keepdims=True)) + 1e-06) * gain
    return scaled.reshape(rows.shape[0], -1).astype(jnp.bfloat16)

def reference(q_video, k_video, v_video, k_stale, v_stale, q_text, k_text, v_text, q_gain, k_gain, out_weight):
    qv = normed(q_video, q_gain)
    qt = normed(q_text, q_gain)
    kf = normed(k_video, k_gain)
    ks = normed(k_stale, k_gain)
    kt = normed(k_text, k_gain)
    width = HEADS * HD

    def block(index):
        vstart = (index * TOK_DEV).astype(jnp.int32)
        tstart = (index * TXT_DEV).astype(jnp.int32)
        queries = jnp.concatenate([lax.dynamic_slice_in_dim(qv, vstart, TOK_DEV, 0), lax.dynamic_slice_in_dim(qt, tstart, TXT_DEV, 0)], axis=0)
        keys = lax.dynamic_update_slice_in_dim(ks, lax.dynamic_slice_in_dim(kf, vstart, TOK_DEV, 0), vstart, 0)
        values = lax.dynamic_update_slice_in_dim(v_stale, lax.dynamic_slice_in_dim(v_video, vstart, TOK_DEV, 0), vstart, 0)
        keys = jnp.concatenate([keys, kt], axis=0)
        values = jnp.concatenate([values, v_text], axis=0)
        q3 = queries.astype(jnp.float32).reshape(-1, HEADS, HD)
        k3 = keys.astype(jnp.float32).reshape(-1, HEADS, HD)
        v3 = values.astype(jnp.float32).reshape(-1, HEADS, HD)
        score = jnp.einsum('rhd,khd->hrk', q3, k3) / jnp.sqrt(jnp.float32(HD))
        top = lax.optimization_barrier(jnp.max(score, axis=-1, keepdims=True))
        expo = jnp.exp(score - top)
        total = lax.optimization_barrier(jnp.sum(expo, axis=-1))
        weight = lax.optimization_barrier(expo.astype(jnp.bfloat16)).astype(jnp.float32)
        summed = jnp.einsum('hrk,khd->rhd', weight, v3)
        attended = summed / jnp.transpose(total)[:, :, None]
        return attended.reshape(-1, width).astype(jnp.bfloat16)
    blocks = lax.map(block, jnp.arange(N_PATCH, dtype=jnp.int32))
    video_rows = blocks[:, :TOK_DEV, :].reshape(-1, width)
    text_rows = blocks[:, TOK_DEV:, :].reshape(-1, width)
    video_out = jnp.dot(video_rows, out_weight, preferred_element_type=jnp.float32).astype(jnp.bfloat16)
    text_out = jnp.dot(text_rows, out_weight, preferred_element_type=jnp.float32).astype(jnp.bfloat16)
    return (video_out, text_out)
```

```python
import functools
import math

import jax
import jax.numpy as jnp
from jax import lax
from jax.experimental import pallas as pl
from jax.experimental.pallas import tpu as pltpu
from jax.sharding import PartitionSpec as P

QUAD = 4
LOW = -1e30
KEY, VALUE, QUERY, FRESH_KEY, FRESH_VALUE = range(5)


def kernel(
    n, tok, txt, size,
    q_video, k_video, v_video, k_stale, v_stale, q_text, k_text, v_text, q_gain, k_gain, w_hbm,
    video_out, text_out,
    rows_f32, outgoing, kv, quad, bias, queries, keybuf, score, acc, total, att_out, att_in, weight,
    send_sem, recv_sem, fwd_send, quad_send, quad_recv, att_send, att_recv, w_sem,
):
    f32, bf16 = jnp.float32, jnp.bfloat16
    pad = outgoing.shape[2]
    part = outgoing.shape[3]
    heads = part // size
    wide = QUAD * pad
    column = n // 2
    quads = column // QUAD
    nblocks = 2 * quads + 1

    me = lax.axis_index("patch")
    plane, side, core = me // 4, (me // 2) % 2, me % 2
    spot = plane * 2 + core
    zz, mine = spot // QUAD, spot % QUAD

    def device(place, at_side):
        return {"patch": ((place // 2) * 2 + at_side) * 2 + place % 2}

    across = device(spot, 1 - side)

    barrier = pltpu.get_barrier_semaphore()

    def greet(d, _):
        pl.semaphore_signal(barrier, inc=1, device_id=device((spot + d) % column, side))
        return 0

    lax.fori_loop(1, column, greet, 0)
    pl.semaphore_signal(barrier, inc=1, device_id=across)
    w_copy = pltpu.make_async_copy(w_hbm, weight, w_sem)
    w_copy.start()
    rows_f32[tok:, :] = jnp.zeros((pad - tok, rows_f32.shape[1]), f32)

    def prepare(kind, video, text, gain):
        if text is not None:
            rows_f32[tok : tok + txt, :] = text[...].astype(f32)
        rows_f32[:tok, :] = video[...].astype(f32)
        for h in range(QUAD * heads):
            x = rows_f32[:, h * size : (h + 1) * size]
            if gain is not None:
                x = x * lax.rsqrt(jnp.mean(x * x, axis=-1, keepdims=True) + 1e-06) * gain[...]
            lane = (h % heads) * size
            outgoing[kind, h // heads, :, lane : lane + size] = x.astype(bf16)

    def distance(i):
        return 1 + (i + column // 2 - 1) % (column - 1)

    def column_copy(kind, i):
        to = (spot + distance(i)) % column
        return pltpu.make_async_remote_copy(
            src_ref=outgoing.at[kind, to % QUAD],
            dst_ref=kv.at[kind, 0, zz, mine],
            send_sem=send_sem.at[kind, i],
            recv_sem=recv_sem.at[kind, 0, spot],
            device_id=device(to, side),
        )

    def column_arrival(kind, from_side, place):
        slot = kv.at[kind, from_side, place // QUAD, place % QUAD]
        return pltpu.make_async_remote_copy(
            src_ref=slot,
            dst_ref=slot,
            send_sem=fwd_send.at[kind, place],
            recv_sem=recv_sem.at[kind, from_side, place],
            device_id=across,
        )

    def forward(kind, place):
        return pltpu.make_async_remote_copy(
            src_ref=kv.at[kind, 0, place // QUAD, place % QUAD],
            dst_ref=kv.at[kind, 1, place // QUAD, place % QUAD],
            send_sem=fwd_send.at[kind, place],
            recv_sem=recv_sem.at[kind, 1, place],
            device_id=across,
        )

    def send_column(kind):
        def go(i, _):
            column_copy(kind, i).start()
            return 0

        kv[kind, 0, zz, mine] = outgoing[kind, mine]
        forward(kind, spot).start()
        lax.fori_loop(0, column - 1, go, 0)

    def quad_copy(kind, e):
        to = (mine + e) % QUAD
        return pltpu.make_async_remote_copy(
            src_ref=outgoing.at[kind, to],
            dst_ref=quad.at[kind - QUERY, mine],
            send_sem=quad_send.at[kind - QUERY, e],
            recv_sem=quad_recv.at[kind - QUERY, mine],
            device_id=device(zz * QUAD + to, side),
        )

    def quad_arrival(kind, e):
        slot = quad.at[kind - QUERY, (mine + e) % QUAD]
        return pltpu.make_async_remote_copy(
            src_ref=slot,
            dst_ref=slot,
            send_sem=quad_send.at[kind - QUERY, e],
            recv_sem=quad_recv.at[kind - QUERY, (mine + e) % QUAD],
            device_id=across,
        )

    def send_quad(kind):
        quad[kind - QUERY, mine] = outgoing[kind, mine]
        for e in range(1, QUAD):
            quad_copy(kind, e).start()

    def wait_and_forward(kind):
        def go(i, _):
            place = (spot + column - distance(i)) % column
            column_arrival(kind, 0, place).wait_recv()
            forward(kind, place).start()
            return 0

        lax.fori_loop(0, column - 1, go, 0)

    prepare(KEY, k_stale, k_text, k_gain)
    pl.semaphore_wait(barrier, column)
    send_column(KEY)
    prepare(QUERY, q_video, q_text, q_gain)
    send_quad(QUERY)
    prepare(FRESH_KEY, k_video, None, k_gain)
    send_quad(FRESH_KEY)
    prepare(VALUE, v_stale, v_text, None)
    send_column(VALUE)
    prepare(FRESH_VALUE, v_video, None, None)
    send_quad(FRESH_VALUE)

    def group(index):
        return sum((index >= pad * g).astype(jnp.int32) for g in range(1, QUAD))

    row = lax.broadcasted_iota(jnp.int32, (wide, wide), 0)
    col = lax.broadcasted_iota(jnp.int32, (wide, wide), 1)
    col_group = group(col)
    same = group(row) == col_group
    inner = col - col_group * pad
    bias[0] = jnp.where(inner >= tok + txt, LOW, 0.0)
    bias[1] = jnp.where((inner >= tok + txt) | (same & (inner < tok)), LOW, 0.0)
    bias[2] = jnp.where(same & (inner < tok), 0.0, LOW)

    wait_and_forward(KEY)
    for kind in (QUERY, FRESH_KEY):
        for e in range(1, QUAD):
            quad_arrival(kind, e).wait_recv()

    for h in range(heads):
        queries[h] = quad[0, :, :, h * size : (h + 1) * size].reshape(wide, size)

    def score_block(b, keys, which):
        for h in range(heads):
            keybuf[h] = keys(h * size)
        for h in range(heads):
            lane = h * size
            s = lax.dot_general(queries[h], keybuf[h], (((1,), (1,)), ((), ())), preferred_element_type=f32)
            score[b, h] = s + bias[which]

    def gathered(kind, from_side, z):
        return lambda lane: kv[kind, from_side, z, :, :, lane : lane + size].reshape(wide, size)

    def exchanged(kind):
        return lambda lane: quad[kind - QUERY, :, :, lane : lane + size].reshape(wide, size)

    score_block(0, exchanged(FRESH_KEY), 2)
    score_block(1, gathered(KEY, 0, zz), 1)

    def own_side(e, _):
        score_block(1 + e, gathered(KEY, 0, (zz + e) % quads), 0)
        return 0

    lax.fori_loop(1, quads, own_side, 0)
    wait_and_forward(VALUE)

    def other_side(e, _):
        z = (zz + e) % quads
        for g in range(QUAD):
            column_arrival(KEY, 1, z * QUAD + g).wait_recv()
        score_block(1 + quads + e, gathered(KEY, 1, z), 0)
        return 0

    lax.fori_loop(0, quads, other_side, 0)

    chunk = 64
    factor = math.log2(math.e) / math.sqrt(size)

    def softmax(i, _):
        h, r = i // (wide // chunk), i % (wide // chunk)
        rows = pl.ds(pl.multiple_of(r * chunk, chunk), chunk)
        top = score[0, h, rows, :]
        for b in range(1, nblocks):
            top = jnp.maximum(top, score[b, h, rows, :])
        top = jnp.max(top, axis=-1, keepdims=True)
        added = jnp.zeros((chunk, wide), f32)
        for b in range(nblocks):
            e = jnp.exp2((score[b, h, rows, :] - top) * factor)
            added = added + e
            score[b, h, rows, :] = e
        total[h, rows, :] = jnp.broadcast_to(jnp.sum(added, axis=-1, keepdims=True), (chunk, size))
        return 0

    lax.fori_loop(0, heads * (wide // chunk), softmax, 0)

    def value_block(b, values, first=False):
        for h in range(heads):
            lane = h * size
            o = jnp.dot(score[b, h].astype(bf16), values(lane), preferred_element_type=f32)
            acc[h] = o if first else acc[h] + o

    for e in range(1, QUAD):
        quad_arrival(FRESH_VALUE, e).wait_recv()
    value_block(0, exchanged(FRESH_VALUE), True)

    def own_values(e, _):
        value_block(1 + e, gathered(VALUE, 0, (zz + e) % quads))
        return 0

    lax.fori_loop(0, quads, own_values, 0)

    def other_values(e, _):
        z = (zz + e) % quads
        for g in range(QUAD):
            column_arrival(VALUE, 1, z * QUAD + g).wait_recv()
        value_block(1 + quads + e, gathered(VALUE, 1, z))
        return 0

    lax.fori_loop(0, quads, other_values, 0)

    for h in range(heads):
        done = (acc[h] / total[h]).astype(bf16)
        att_out[:, :, h * size : (h + 1) * size] = done.reshape(QUAD, pad, size)

    def att_copy(e):
        to = (mine + e) % QUAD
        return pltpu.make_async_remote_copy(
            src_ref=att_out.at[to],
            dst_ref=att_in.at[mine],
            send_sem=att_send.at[e],
            recv_sem=att_recv.at[mine],
            device_id=device(zz * QUAD + to, side),
        )

    def att_arrival(e):
        slot = att_in.at[(mine + e) % QUAD]
        return pltpu.make_async_remote_copy(
            src_ref=slot,
            dst_ref=slot,
            send_sem=att_send.at[e],
            recv_sem=att_recv.at[(mine + e) % QUAD],
            device_id=across,
        )

    for e in range(1, QUAD):
        att_copy(e).start()
    att_in[mine] = att_out[mine]
    w_copy.wait()
    for e in range(1, QUAD):
        att_arrival(e).wait_recv()

    step = 512
    attended = jnp.concatenate([att_in[g] for g in range(QUAD)], axis=1)

    def project(i, _):
        cols = pl.ds(pl.multiple_of(i * step, step), step)
        o = jnp.dot(attended, weight[:, cols], preferred_element_type=f32)
        video_out[:, cols] = o[:tok].astype(bf16)
        text_out[:, cols] = o[tok : tok + txt].astype(bf16)
        return 0

    lax.fori_loop(0, weight.shape[1] // step, project, 0)

    def finish(i, _):
        for kind in (KEY, VALUE):
            column_copy(kind, i).wait_send()
            forward(kind, i).wait_send()
        return 0

    lax.fori_loop(0, column - 1, finish, 0)
    for kind in (KEY, VALUE):
        forward(kind, column - 1).wait_send()
    for e in range(1, QUAD):
        for kind in (QUERY, FRESH_KEY, FRESH_VALUE):
            quad_copy(kind, e).wait_send()
        att_copy(e).wait_send()


def solution(mesh):
    n = mesh.shape["patch"]

    def body(*args):
        q_video, q_text, q_gain, weight = args[0], args[5], args[8], args[10]
        tok, width = q_video.shape
        txt, size = q_text.shape[0], q_gain.shape[0]
        pad = -(-(tok + txt) // 16) * 16
        part = width // QUAD
        heads = part // size
        column = n // 2
        quads = column // QUAD
        nblocks = 2 * quads + 1
        wide = QUAD * pad
        out = weight.shape[1]
        bf16, f32 = jnp.bfloat16, jnp.float32
        vmem = pl.BlockSpec(memory_space=pltpu.VMEM)
        dma = pltpu.SemaphoreType.DMA
        args = list(args)
        args[8], args[9] = args[8].reshape(1, size), args[9].reshape(1, size)
        return pl.pallas_call(
            functools.partial(kernel, n, tok, txt, size),
            out_shape=(
                jax.ShapeDtypeStruct((tok, out), bf16),
                jax.ShapeDtypeStruct((txt, out), bf16),
            ),
            in_specs=[vmem] * 10 + [pl.BlockSpec(memory_space=pl.ANY)],
            out_specs=(vmem, vmem),
            scratch_shapes=[
                pltpu.VMEM((pad, width), f32),
                pltpu.VMEM((5, QUAD, pad, part), bf16),
                pltpu.VMEM((2, 2, quads, QUAD, pad, part), bf16),
                pltpu.VMEM((3, QUAD, pad, part), bf16),
                pltpu.VMEM((3, wide, wide), f32),
                pltpu.VMEM((heads, wide, size), bf16),
                pltpu.VMEM((heads, wide, size), bf16),
                pltpu.VMEM((nblocks, heads, wide, wide), f32),
                pltpu.VMEM((heads, wide, size), f32),
                pltpu.VMEM((heads, wide, size), f32),
                pltpu.VMEM((QUAD, pad, part), bf16),
                pltpu.VMEM((QUAD, pad, part), bf16),
                pltpu.VMEM(weight.shape, bf16),
                dma((2, column)),
                dma((2, 2, column)),
                dma((2, column)),
                dma((3, QUAD)),
                dma((3, QUAD)),
                dma((QUAD,)),
                dma((QUAD,)),
                dma,
            ],
            compiler_params=pltpu.CompilerParams(
                collective_id=0, has_side_effects=True, vmem_limit_bytes=60 * 1024 * 1024
            ),
        )(*args)

    rows = P(("clips", "patch"), None)
    return jax.shard_map(
        body,
        mesh=mesh,
        in_specs=(rows,) * 8 + (P(),) * 3,
        out_specs=(rows, rows),
        check_vma=False,
    )
```

```python
import functools
import math

import jax
import jax.numpy as jnp
from jax import lax
from jax.experimental import pallas as pl
from jax.experimental.pallas import tpu as pltpu
from jax.sharding import PartitionSpec as P

QUAD = 4
LOW = -1e30
KEY, VALUE, QUERY, FRESH_KEY, FRESH_VALUE = range(5)


def kernel(
    n, tok, txt, size,
    q_video, k_video, v_video, k_stale, v_stale, q_text, k_text, v_text, q_gain, k_gain, w_hbm,
    out,
    rows_f32, partial, outgoing, kv, quad, bias, queries, keybuf, score, acc, total, att_out, att_in, weight,
    send_sem, recv_sem, fwd_send, quad_send, quad_recv, att_send, att_recv, w_sem,
):
    f32, bf16 = jnp.float32, jnp.bfloat16
    pad = outgoing.shape[2]
    part = outgoing.shape[3]
    heads = part // size
    wide = QUAD * pad
    column = n // 2
    quads = column // QUAD
    nblocks = 2 * quads + 1

    me = lax.axis_index("patch")
    plane, side, core = me // 4, (me // 2) % 2, me % 2
    spot = plane * 2 + core
    zz, mine = spot // QUAD, spot % QUAD

    def device(place, at_side):
        return {"patch": ((place // 2) * 2 + at_side) * 2 + place % 2}

    across = device(spot, 1 - side)

    barrier = pltpu.get_barrier_semaphore()

    def greet(d, _):
        pl.semaphore_signal(barrier, inc=1, device_id=device((spot + d) % column, side))
        return 0

    lax.fori_loop(1, column, greet, 0)
    pl.semaphore_signal(barrier, inc=1, device_id=across)
    w_copy = pltpu.make_async_copy(w_hbm, weight, w_sem)
    w_copy.start()
    rows_f32[tok:, :] = jnp.zeros((pad - tok, rows_f32.shape[1]), f32)

    def prepare(kind, video, text, gain):
        if text is not None:
            rows_f32[tok : tok + txt, :] = text[...].astype(f32)
        rows_f32[:tok, :] = video[...].astype(f32)
        for h in range(QUAD * heads):
            x = rows_f32[:, h * size : (h + 1) * size]
            if gain is not None:
                x = x * lax.rsqrt(jnp.mean(x * x, axis=-1, keepdims=True) + 1e-06) * gain[...]
            lane = (h % heads) * size
            outgoing[kind, h // heads, :, lane : lane + size] = x.astype(bf16)

    planes = column // 2
    partner_place = plane * 2 + 1 - core

    def outward(i):
        away = 1 + (i // 2 + planes // 2 - 1) % (planes - 1)
        return ((plane + away) % planes) * 2 + (core + i) % 2

    def inward(i):
        away = 1 + (i // 2 + planes // 2 - 1) % (planes - 1)
        return ((plane + planes - away) % planes) * 2 + (core + i) % 2

    def column_copy(kind, to):
        return pltpu.make_async_remote_copy(
            src_ref=outgoing.at[kind, to % QUAD],
            dst_ref=kv.at[kind, 0, zz, mine],
            send_sem=send_sem.at[kind, to],
            recv_sem=recv_sem.at[kind, 0, spot],
            device_id=device(to, side),
        )

    def column_arrival(kind, from_side, place):
        slot = kv.at[kind, from_side, place // QUAD, place % QUAD]
        return pltpu.make_async_remote_copy(
            src_ref=slot,
            dst_ref=slot,
            send_sem=fwd_send.at[kind, place],
            recv_sem=recv_sem.at[kind, from_side, place],
            device_id=across,
        )

    def forward(kind, place):
        return pltpu.make_async_remote_copy(
            src_ref=kv.at[kind, 0, place // QUAD, place % QUAD],
            dst_ref=kv.at[kind, 1, place // QUAD, place % QUAD],
            send_sem=fwd_send.at[kind, place],
            recv_sem=recv_sem.at[kind, 1, place],
            device_id=across,
        )

    def send_column(kind):
        def go(i, _):
            column_copy(kind, outward(i)).start()
            return 0

        column_copy(kind, partner_place).start()
        kv[kind, 0, zz, mine] = outgoing[kind, mine]
        forward(kind, spot).start()
        lax.fori_loop(0, column - 2, go, 0)

    def quad_copy(kind, e):
        to = (mine + e) % QUAD
        return pltpu.make_async_remote_copy(
            src_ref=outgoing.at[kind, to],
            dst_ref=quad.at[kind - QUERY, mine],
            send_sem=quad_send.at[kind - QUERY, e],
            recv_sem=quad_recv.at[kind - QUERY, mine],
            device_id=device(zz * QUAD + to, side),
        )

    def quad_arrival(kind, e):
        slot = quad.at[kind - QUERY, (mine + e) % QUAD]
        return pltpu.make_async_remote_copy(
            src_ref=slot,
            dst_ref=slot,
            send_sem=quad_send.at[kind - QUERY, e],
            recv_sem=quad_recv.at[kind - QUERY, (mine + e) % QUAD],
            device_id=across,
        )

    def send_quad(kind):
        quad[kind - QUERY, mine] = outgoing[kind, mine]
        for e in range(1, QUAD):
            quad_copy(kind, e).start()

    def wait_and_forward(kind):
        def go(i, _):
            place = inward(i)
            column_arrival(kind, 0, place).wait_recv()
            forward(kind, place).start()
            return 0

        column_arrival(kind, 0, partner_place).wait_recv()
        forward(kind, partner_place).start()
        lax.fori_loop(0, column - 2, go, 0)

    prepare(KEY, k_stale, k_text, k_gain)
    pl.semaphore_wait(barrier, column)
    send_column(KEY)
    prepare(QUERY, q_video, q_text, q_gain)
    send_quad(QUERY)
    prepare(FRESH_KEY, k_video, None, k_gain)
    send_quad(FRESH_KEY)
    prepare(VALUE, v_stale, v_text, None)
    send_column(VALUE)
    prepare(FRESH_VALUE, v_video, None, None)
    send_quad(FRESH_VALUE)

    def group(index):
        return sum((index >= pad * g).astype(jnp.int32) for g in range(1, QUAD))

    row = lax.broadcasted_iota(jnp.int32, (wide, wide), 0)
    col = lax.broadcasted_iota(jnp.int32, (wide, wide), 1)
    col_group = group(col)
    same = group(row) == col_group
    inner = col - col_group * pad
    bias[0] = jnp.where(inner >= tok + txt, LOW, 0.0)
    bias[1] = jnp.where((inner >= tok + txt) | (same & (inner < tok)), LOW, 0.0)
    bias[2] = jnp.where(same & (inner < tok), 0.0, LOW)

    wait_and_forward(KEY)
    for kind in (QUERY, FRESH_KEY):
        for e in range(1, QUAD):
            quad_arrival(kind, e).wait_recv()

    for h in range(heads):
        queries[h] = quad[0, :, :, h * size : (h + 1) * size].reshape(wide, size)

    def score_block(b, keys, which):
        for h in range(heads):
            keybuf[h] = keys(h * size)
        for h in range(heads):
            lane = h * size
            s = lax.dot_general(queries[h], keybuf[h], (((1,), (1,)), ((), ())), preferred_element_type=f32)
            score[b, h] = s + bias[which]

    def gathered(kind, from_side, z):
        return lambda lane: kv[kind, from_side, z, :, :, lane : lane + size].reshape(wide, size)

    def exchanged(kind):
        return lambda lane: quad[kind - QUERY, :, :, lane : lane + size].reshape(wide, size)

    score_block(0, exchanged(FRESH_KEY), 2)
    score_block(1, gathered(KEY, 0, zz), 1)

    def own_side(e, _):
        score_block(1 + e, gathered(KEY, 0, (zz + e) % quads), 0)
        return 0

    lax.fori_loop(1, quads, own_side, 0)
    wait_and_forward(VALUE)

    def other_side(e, _):
        z = (zz + e) % quads
        for g in range(QUAD):
            column_arrival(KEY, 1, z * QUAD + g).wait_recv()
        score_block(1 + quads + e, gathered(KEY, 1, z), 0)
        return 0

    lax.fori_loop(0, quads, other_side, 0)

    chunk = 64
    factor = math.log2(math.e) / math.sqrt(size)

    def softmax(i, _):
        h, r = i // (wide // chunk), i % (wide // chunk)
        rows = pl.ds(pl.multiple_of(r * chunk, chunk), chunk)
        top = score[0, h, rows, :]
        for b in range(1, nblocks):
            top = jnp.maximum(top, score[b, h, rows, :])
        top = jnp.max(top, axis=-1, keepdims=True)
        added = jnp.zeros((chunk, wide), f32)
        for b in range(nblocks):
            e = jnp.exp2((score[b, h, rows, :] - top) * factor)
            added = added + e
            score[b, h, rows, :] = e
        total[h, rows, :] = jnp.broadcast_to(jnp.sum(added, axis=-1, keepdims=True), (chunk, size))
        return 0

    lax.fori_loop(0, heads * (wide // chunk), softmax, 0)

    def value_block(b, values, first=False):
        for h in range(heads):
            lane = h * size
            o = jnp.dot(score[b, h].astype(bf16), values(lane), preferred_element_type=f32)
            acc[h] = o if first else acc[h] + o

    for e in range(1, QUAD):
        quad_arrival(FRESH_VALUE, e).wait_recv()
    value_block(0, exchanged(FRESH_VALUE), True)

    def own_values(e, _):
        value_block(1 + e, gathered(VALUE, 0, (zz + e) % quads))
        return 0

    lax.fori_loop(0, quads, own_values, 0)

    def other_values(e, _):
        z = (zz + e) % quads
        for g in range(QUAD):
            column_arrival(VALUE, 1, z * QUAD + g).wait_recv()
        value_block(1 + quads + e, gathered(VALUE, 1, z))
        return 0

    lax.fori_loop(0, quads, other_values, 0)

    for h in range(heads):
        done = (acc[h] / total[h]).astype(bf16)
        att_out[:, :, h * size : (h + 1) * size] = done.reshape(QUAD, pad, size)

    def att_copy(e):
        to = (mine + e) % QUAD
        return pltpu.make_async_remote_copy(
            src_ref=att_out.at[to],
            dst_ref=att_in.at[mine],
            send_sem=att_send.at[e],
            recv_sem=att_recv.at[mine],
            device_id=device(zz * QUAD + to, side),
        )

    for e in range(1, QUAD):
        att_copy(e).start()
    att_in[mine] = att_out[mine]
    w_copy.wait()
    step = 512
    half = mine // 2

    def att_wait(place):
        slot = att_in.at[place]
        pltpu.make_async_remote_copy(
            src_ref=slot, dst_ref=slot, send_sem=att_send.at[0], recv_sem=att_recv.at[place], device_id=across
        ).wait_recv()

    def project(which, last):
        attended = jnp.concatenate([att_in[which * 2], att_in[which * 2 + 1]], axis=1)
        depth = pl.ds(pl.multiple_of(which * 2 * part, 2 * part), 2 * part)

        def go(i, _):
            cols = pl.ds(pl.multiple_of(i * step, step), step)
            o = jnp.dot(attended, weight[depth, cols], preferred_element_type=f32)
            if last:
                out[:, cols] = (partial[:, cols] + o).astype(bf16)
            else:
                partial[:, cols] = o
            return 0

        lax.fori_loop(0, weight.shape[1] // step, go, 0)

    att_wait(half * 2 + 1 - core)
    project(half, False)
    for g in range(2):
        att_wait((1 - half) * 2 + g)
    project(1 - half, True)

    def finish(i, _):
        for kind in (KEY, VALUE):
            column_copy(kind, outward(i)).wait_send()
            forward(kind, outward(i)).wait_send()
        return 0

    lax.fori_loop(0, column - 2, finish, 0)
    for kind in (KEY, VALUE):
        column_copy(kind, partner_place).wait_send()
        forward(kind, partner_place).wait_send()
        forward(kind, spot).wait_send()
    for e in range(1, QUAD):
        for kind in (QUERY, FRESH_KEY, FRESH_VALUE):
            quad_copy(kind, e).wait_send()
        att_copy(e).wait_send()


def split(tok, both, video_out, text_out):
    video_out[...] = both[:tok]
    text_out[...] = both[tok : tok + text_out.shape[0]]


def solution(mesh):
    n = mesh.shape["patch"]

    def body(*args):
        q_video, q_text, q_gain, weight = args[0], args[5], args[8], args[10]
        tok, width = q_video.shape
        txt, size = q_text.shape[0], q_gain.shape[0]
        pad = -(-(tok + txt) // 16) * 16
        part = width // QUAD
        heads = part // size
        column = n // 2
        quads = column // QUAD
        nblocks = 2 * quads + 1
        wide = QUAD * pad
        out = weight.shape[1]
        bf16, f32 = jnp.bfloat16, jnp.float32
        vmem = pl.BlockSpec(memory_space=pltpu.VMEM)
        dma = pltpu.SemaphoreType.DMA
        args = list(args)
        args[8], args[9] = args[8].reshape(1, size), args[9].reshape(1, size)
        both = pl.pallas_call(
            functools.partial(kernel, n, tok, txt, size),
            out_shape=jax.ShapeDtypeStruct((pad, out), bf16),
            in_specs=[vmem] * 10 + [pl.BlockSpec(memory_space=pl.ANY)],
            out_specs=vmem,
            scratch_shapes=[
                pltpu.VMEM((pad, width), f32),
                pltpu.VMEM((pad, out), f32),
                pltpu.VMEM((5, QUAD, pad, part), bf16),
                pltpu.VMEM((2, 2, quads, QUAD, pad, part), bf16),
                pltpu.VMEM((3, QUAD, pad, part), bf16),
                pltpu.VMEM((3, wide, wide), f32),
                pltpu.VMEM((heads, wide, size), bf16),
                pltpu.VMEM((heads, wide, size), bf16),
                pltpu.VMEM((nblocks, heads, wide, wide), f32),
                pltpu.VMEM((heads, wide, size), f32),
                pltpu.VMEM((heads, wide, size), f32),
                pltpu.VMEM((QUAD, pad, part), bf16),
                pltpu.VMEM((QUAD, pad, part), bf16),
                pltpu.VMEM(weight.shape, bf16),
                dma((2, column)),
                dma((2, 2, column)),
                dma((2, column)),
                dma((3, QUAD)),
                dma((3, QUAD)),
                dma((QUAD,)),
                dma((QUAD,)),
                dma,
            ],
            compiler_params=pltpu.CompilerParams(
                collective_id=0, has_side_effects=True, vmem_limit_bytes=60 * 1024 * 1024
            ),
        )(*args)
        return pl.pallas_call(
            functools.partial(split, tok),
            out_shape=(
                jax.ShapeDtypeStruct((tok, out), bf16),
                jax.ShapeDtypeStruct((txt, out), bf16),
            ),
            in_specs=[vmem],
            out_specs=(vmem, vmem),
        )(both)

    rows = P(("clips", "patch"), None)
    return jax.shard_map(
        body,
        mesh=mesh,
        in_specs=(rows,) * 8 + (P(),) * 3,
        out_specs=(rows, rows),
        check_vma=False,
    )
```

```python
import functools
import math

import jax
import jax.numpy as jnp
from jax import lax
from jax.experimental import pallas as pl
from jax.experimental.pallas import tpu as pltpu
from jax.sharding import PartitionSpec as P

QUAD = 4
LOW = -1e30
KEY, VALUE, QUERY, FRESH_KEY, FRESH_VALUE = range(5)


def kernel(
    n, tok, txt, size,
    q_video, k_video, v_video, k_stale, v_stale, q_text, k_text, v_text, q_gain, k_gain, w_hbm,
    out,
    rows_f32, partial, outgoing, kv, quad, bias, queries, keybuf, score, acc, total, att_out, att_in, weight,
    send_sem, recv_sem, fwd_send, quad_send, quad_recv, att_send, att_recv, w_sem,
):
    f32, bf16 = jnp.float32, jnp.bfloat16
    pad = outgoing.shape[2]
    part = outgoing.shape[3]
    heads = part // size
    wide = QUAD * pad
    column = n // 2
    quads = column // QUAD
    nblocks = 2 * quads + 1

    me = lax.axis_index("patch")
    plane, side, core = me // 4, (me // 2) % 2, me % 2
    spot = plane * 2 + core
    zz, mine = spot // QUAD, spot % QUAD

    def device(place, at_side):
        return {"patch": ((place // 2) * 2 + at_side) * 2 + place % 2}

    across = device(spot, 1 - side)

    barrier = pltpu.get_barrier_semaphore()

    def greet(d, _):
        pl.semaphore_signal(barrier, inc=1, device_id=device((spot + d) % column, side))
        return 0

    lax.fori_loop(1, column, greet, 0)
    pl.semaphore_signal(barrier, inc=1, device_id=across)
    w_copy = pltpu.make_async_copy(w_hbm, weight, w_sem)
    w_copy.start()
    rows_f32[tok:, :] = jnp.zeros((pad - tok, rows_f32.shape[1]), f32)

    def prepare(kind, video, text, gain):
        if text is not None:
            rows_f32[tok : tok + txt, :] = text[...].astype(f32)
        rows_f32[:tok, :] = video[...].astype(f32)
        for h in range(QUAD * heads):
            x = rows_f32[:, h * size : (h + 1) * size]
            if gain is not None:
                x = x * lax.rsqrt(jnp.mean(x * x, axis=-1, keepdims=True) + 1e-06) * gain[...]
            lane = (h % heads) * size
            outgoing[kind, h // heads, :, lane : lane + size] = x.astype(bf16)

    planes = column // 2
    partner_place = plane * 2 + 1 - core

    def outward(i):
        away = 1 + (i // 2 + planes // 2 - 1) % (planes - 1)
        return ((plane + away) % planes) * 2 + (core + i) % 2

    def inward(i):
        away = 1 + (i // 2 + planes // 2 - 1) % (planes - 1)
        return ((plane + planes - away) % planes) * 2 + (core + i) % 2

    def column_copy(kind, to):
        return pltpu.make_async_remote_copy(
            src_ref=outgoing.at[kind, to % QUAD],
            dst_ref=kv.at[kind, 0, zz, mine],
            send_sem=send_sem.at[kind, to],
            recv_sem=recv_sem.at[kind, 0, spot],
            device_id=device(to, side),
        )

    def column_arrival(kind, from_side, place):
        slot = kv.at[kind, from_side, place // QUAD, place % QUAD]
        return pltpu.make_async_remote_copy(
            src_ref=slot,
            dst_ref=slot,
            send_sem=fwd_send.at[kind, place],
            recv_sem=recv_sem.at[kind, from_side, place],
            device_id=across,
        )

    def forward(kind, place):
        return pltpu.make_async_remote_copy(
            src_ref=kv.at[kind, 0, place // QUAD, place % QUAD],
            dst_ref=kv.at[kind, 1, place // QUAD, place % QUAD],
            send_sem=fwd_send.at[kind, place],
            recv_sem=recv_sem.at[kind, 1, place],
            device_id=across,
        )

    def send_column(kind):
        def go(i, _):
            column_copy(kind, outward(i)).start()
            return 0

        column_copy(kind, partner_place).start()
        kv[kind, 0, zz, mine] = outgoing[kind, mine]
        forward(kind, spot).start()
        lax.fori_loop(0, column - 2, go, 0)

    def quad_copy(kind, e):
        to = (mine + e) % QUAD
        return pltpu.make_async_remote_copy(
            src_ref=outgoing.at[kind, to],
            dst_ref=quad.at[kind - QUERY, mine],
            send_sem=quad_send.at[kind - QUERY, e],
            recv_sem=quad_recv.at[kind - QUERY, mine],
            device_id=device(zz * QUAD + to, side),
        )

    def quad_arrival(kind, e):
        slot = quad.at[kind - QUERY, (mine + e) % QUAD]
        return pltpu.make_async_remote_copy(
            src_ref=slot,
            dst_ref=slot,
            send_sem=quad_send.at[kind - QUERY, e],
            recv_sem=quad_recv.at[kind - QUERY, (mine + e) % QUAD],
            device_id=across,
        )

    def send_quad(kind):
        quad[kind - QUERY, mine] = outgoing[kind, mine]
        for e in range(1, QUAD):
            quad_copy(kind, e).start()

    def wait_and_forward(kind):
        def go(i, _):
            place = inward(i)
            column_arrival(kind, 0, place).wait_recv()
            forward(kind, place).start()
            return 0

        column_arrival(kind, 0, partner_place).wait_recv()
        forward(kind, partner_place).start()
        lax.fori_loop(0, column - 2, go, 0)

    prepare(KEY, k_stale, k_text, k_gain)
    pl.semaphore_wait(barrier, column)
    send_column(KEY)
    prepare(QUERY, q_video, q_text, q_gain)
    send_quad(QUERY)
    prepare(FRESH_KEY, k_video, None, k_gain)
    send_quad(FRESH_KEY)
    prepare(VALUE, v_stale, v_text, None)
    send_column(VALUE)
    prepare(FRESH_VALUE, v_video, None, None)
    send_quad(FRESH_VALUE)

    def group(index):
        return sum((index >= pad * g).astype(jnp.int32) for g in range(1, QUAD))

    row = lax.broadcasted_iota(jnp.int32, (wide, wide), 0)
    col = lax.broadcasted_iota(jnp.int32, (wide, wide), 1)
    col_group = group(col)
    same = group(row) == col_group
    inner = col - col_group * pad
    bias[0] = jnp.where(inner >= tok + txt, LOW, 0.0)
    bias[1] = jnp.where((inner >= tok + txt) | (same & (inner < tok)), LOW, 0.0)
    bias[2] = jnp.where(same & (inner < tok), 0.0, LOW)

    wait_and_forward(KEY)
    for kind in (QUERY, FRESH_KEY):
        for e in range(1, QUAD):
            quad_arrival(kind, e).wait_recv()

    for h in range(heads):
        queries[h] = quad[0, :, :, h * size : (h + 1) * size].reshape(wide, size)

    def score_block(b, keys, which):
        for h in range(heads):
            keybuf[h] = keys(h * size)
        for h in range(heads):
            lane = h * size
            s = lax.dot_general(queries[h], keybuf[h], (((1,), (1,)), ((), ())), preferred_element_type=f32)
            score[b, h] = s + bias[which]

    def gathered(kind, from_side, z):
        return lambda lane: kv[kind, from_side, z, :, :, lane : lane + size].reshape(wide, size)

    def exchanged(kind):
        return lambda lane: quad[kind - QUERY, :, :, lane : lane + size].reshape(wide, size)

    score_block(0, exchanged(FRESH_KEY), 2)
    score_block(1, gathered(KEY, 0, zz), 1)

    def own_side(e, _):
        score_block(1 + e, gathered(KEY, 0, (zz + e) % quads), 0)
        return 0

    lax.fori_loop(1, quads, own_side, 0)
    wait_and_forward(VALUE)

    def other_side(e, _):
        z = (zz + e) % quads
        for g in range(QUAD):
            column_arrival(KEY, 1, z * QUAD + g).wait_recv()
        score_block(1 + quads + e, gathered(KEY, 1, z), 0)
        return 0

    lax.fori_loop(0, quads, other_side, 0)

    chunk = 64
    factor = math.log2(math.e) / math.sqrt(size)

    def softmax(i, _):
        h, r = i // (wide // chunk), i % (wide // chunk)
        rows = pl.ds(pl.multiple_of(r * chunk, chunk), chunk)
        top = score[0, h, rows, :]
        for b in range(1, nblocks):
            top = jnp.maximum(top, score[b, h, rows, :])
        top = jnp.max(top, axis=-1, keepdims=True)
        added = jnp.zeros((chunk, wide), f32)
        for b in range(nblocks):
            e = jnp.exp2((score[b, h, rows, :] - top) * factor)
            added = added + e
            score[b, h, rows, :] = e
        total[h, rows, :] = jnp.broadcast_to(jnp.sum(added, axis=-1, keepdims=True), (chunk, size))
        return 0

    lax.fori_loop(0, heads * (wide // chunk), softmax, 0)

    def value_block(b, values, first=False):
        for h in range(heads):
            lane = h * size
            o = jnp.dot(score[b, h].astype(bf16), values(lane), preferred_element_type=f32)
            acc[h] = o if first else acc[h] + o

    value_block(1, gathered(VALUE, 0, zz), True)

    def own_values(e, _):
        value_block(1 + e, gathered(VALUE, 0, (zz + e) % quads))
        return 0

    lax.fori_loop(1, quads, own_values, 0)
    for e in range(1, QUAD):
        quad_arrival(FRESH_VALUE, e).wait_recv()
    value_block(0, exchanged(FRESH_VALUE))

    def other_values(e, _):
        z = (zz + e) % quads
        for g in range(QUAD):
            column_arrival(VALUE, 1, z * QUAD + g).wait_recv()
        value_block(1 + quads + e, gathered(VALUE, 1, z))
        return 0

    lax.fori_loop(0, quads, other_values, 0)

    for h in range(heads):
        done = (acc[h] / total[h]).astype(bf16)
        att_out[:, :, h * size : (h + 1) * size] = done.reshape(QUAD, pad, size)

    def att_copy(e):
        to = (mine + e) % QUAD
        return pltpu.make_async_remote_copy(
            src_ref=att_out.at[to],
            dst_ref=att_in.at[mine],
            send_sem=att_send.at[e],
            recv_sem=att_recv.at[mine],
            device_id=device(zz * QUAD + to, side),
        )

    for e in range(1, QUAD):
        att_copy(e).start()
    att_in[mine] = att_out[mine]
    w_copy.wait()
    step = 512
    half = mine // 2

    def att_wait(place):
        slot = att_in.at[place]
        pltpu.make_async_remote_copy(
            src_ref=slot, dst_ref=slot, send_sem=att_send.at[0], recv_sem=att_recv.at[place], device_id=across
        ).wait_recv()

    def project(which, last):
        attended = jnp.concatenate([att_in[which * 2], att_in[which * 2 + 1]], axis=1)
        depth = pl.ds(pl.multiple_of(which * 2 * part, 2 * part), 2 * part)

        def go(i, _):
            cols = pl.ds(pl.multiple_of(i * step, step), step)
            o = jnp.dot(attended, weight[depth, cols], preferred_element_type=f32)
            if last:
                out[:, cols] = (partial[:, cols] + o).astype(bf16)
            else:
                partial[:, cols] = o
            return 0

        lax.fori_loop(0, weight.shape[1] // step, go, 0)

    att_wait(half * 2 + 1 - core)
    project(half, False)
    for g in range(2):
        att_wait((1 - half) * 2 + g)
    project(1 - half, True)

    def finish(i, _):
        for kind in (KEY, VALUE):
            column_copy(kind, outward(i)).wait_send()
            forward(kind, outward(i)).wait_send()
        return 0

    lax.fori_loop(0, column - 2, finish, 0)
    for kind in (KEY, VALUE):
        column_copy(kind, partner_place).wait_send()
        forward(kind, partner_place).wait_send()
        forward(kind, spot).wait_send()
    for e in range(1, QUAD):
        for kind in (QUERY, FRESH_KEY, FRESH_VALUE):
            quad_copy(kind, e).wait_send()
        att_copy(e).wait_send()


def split(tok, both, video_out, text_out):
    video_out[...] = both[:tok]
    text_out[...] = both[tok : tok + text_out.shape[0]]


def solution(mesh):
    n = mesh.shape["patch"]

    def body(*args):
        q_video, q_text, q_gain, weight = args[0], args[5], args[8], args[10]
        tok, width = q_video.shape
        txt, size = q_text.shape[0], q_gain.shape[0]
        pad = -(-(tok + txt) // 16) * 16
        part = width // QUAD
        heads = part // size
        column = n // 2
        quads = column // QUAD
        nblocks = 2 * quads + 1
        wide = QUAD * pad
        out = weight.shape[1]
        bf16, f32 = jnp.bfloat16, jnp.float32
        vmem = pl.BlockSpec(memory_space=pltpu.VMEM)
        dma = pltpu.SemaphoreType.DMA
        args = list(args)
        args[8], args[9] = args[8].reshape(1, size), args[9].reshape(1, size)
        both = pl.pallas_call(
            functools.partial(kernel, n, tok, txt, size),
            out_shape=jax.ShapeDtypeStruct((pad, out), bf16),
            in_specs=[vmem] * 10 + [pl.BlockSpec(memory_space=pl.ANY)],
            out_specs=vmem,
            scratch_shapes=[
                pltpu.VMEM((pad, width), f32),
                pltpu.VMEM((pad, out), f32),
                pltpu.VMEM((5, QUAD, pad, part), bf16),
                pltpu.VMEM((2, 2, quads, QUAD, pad, part), bf16),
                pltpu.VMEM((3, QUAD, pad, part), bf16),
                pltpu.VMEM((3, wide, wide), f32),
                pltpu.VMEM((heads, wide, size), bf16),
                pltpu.VMEM((heads, wide, size), bf16),
                pltpu.VMEM((nblocks, heads, wide, wide), f32),
                pltpu.VMEM((heads, wide, size), f32),
                pltpu.VMEM((heads, wide, size), f32),
                pltpu.VMEM((QUAD, pad, part), bf16),
                pltpu.VMEM((QUAD, pad, part), bf16),
                pltpu.VMEM(weight.shape, bf16),
                dma((2, column)),
                dma((2, 2, column)),
                dma((2, column)),
                dma((3, QUAD)),
                dma((3, QUAD)),
                dma((QUAD,)),
                dma((QUAD,)),
                dma,
            ],
            compiler_params=pltpu.CompilerParams(
                collective_id=0, has_side_effects=True, vmem_limit_bytes=60 * 1024 * 1024
            ),
        )(*args)
        return pl.pallas_call(
            functools.partial(split, tok),
            out_shape=(
                jax.ShapeDtypeStruct((tok, out), bf16),
                jax.ShapeDtypeStruct((txt, out), bf16),
            ),
            in_specs=[vmem],
            out_specs=(vmem, vmem),
        )(both)

    rows = P(("clips", "patch"), None)
    return jax.shard_map(
        body,
        mesh=mesh,
        in_specs=(rows,) * 8 + (P(),) * 3,
        out_specs=(rows, rows),
        check_vma=False,
    )
```
